768 devices in a mesh: group: 12 (over z_lo, core), blk: 64 (over y, x, z_hi).
Axes of the slice: x: 4, y: 8, z: 12 (z_hi: 2, z_lo: 6; z = z_hi * 6 + z_lo), core: 2. Of those that a mesh axis runs over, the one named last changes fastest.
Arguments:
- image_embed: bfloat16 [294912, 1024], P(('group', 'blk')), may hold values from -0.25 to 0.25
- text_embed: bfloat16 [294912, 1024], P(('group', 'blk')), may hold values from -0.25 to 0.25
- positive_partner_index: int32 [294912], P(('group', 'blk')), may hold values from 0 to 294911, as said below
- exponent_of_multiplier: float32 [1], replicated, may hold values from 1 to 2
- logit_bias: float32 [1], replicated, may hold values from -4 to -1
Outputs:
- image_grad: float32 [294912, 1024], P(('group', 'blk'))
- text_grad: float32 [294912, 1024], P(('group', 'blk'))
The draws below stay inside these ranges and needn't reach their ends.
Inputs may be any that keep to these rules, and one draw needn't show every extreme that they name: `positive_partner_index`: each row names a row of one of the four text blocks that its image block is scored against.
All inputs are finite; a program needn't handle non-finite values.
Results may differ from the reference program's by a relative error of at most 0.0039.
Values may be sent and summed in bfloat16 or wider, within the bound.
No kernel may reach another device: no remote copies, remote signals or barrier semaphores. Data moves between devices by JAX's collectives and lax.ppermute only.
A program may use at most 32 MiB of HBM per device.

```python
import jax
import jax.numpy as jnp
from jax import lax

D = 1024
ROWS = 384
CYCLE = 64
GROUPS = 12
TOKENS = 294912


def draw_positive_partner_index(key, part):
    key = jax.random.fold_in(key, 7)
    first_key, second_key = jax.random.split(key)
    row_index = jnp.arange(TOKENS, dtype=jnp.int32)
    block_index = row_index // ROWS
    group_of = block_index // CYCLE
    cycle_of = block_index % CYCLE
    pick_block = jax.random.randint(first_key, (TOKENS,), 0, 4, dtype=jnp.int32)
    text_group = jnp.where(pick_block == 3, (group_of + GROUPS - 1) % GROUPS, group_of)
    text_cycle = jnp.where(pick_block == 1, (cycle_of + CYCLE - 1) % CYCLE, jnp.where(pick_block == 2, (cycle_of + CYCLE - 2) % CYCLE, cycle_of))
    within = jax.random.randint(second_key, (TOKENS,), 0, ROWS, dtype=jnp.int32)
    return ((text_group * CYCLE + text_cycle) * ROWS + within).astype(jnp.int32)


def level_of(rng, shape, pieces, smallest, largest):
    factor_of = 1.0
    for dim, blocks in pieces:
        steps = jax.random.uniform(jax.random.fold_in(jax.random.fold_in(rng, 6), dim), (blocks,), jnp.float32, smallest / len(pieces), largest / len(pieces))
        factor_of = factor_of * jnp.repeat(jnp.exp(steps), shape[dim] // blocks).reshape((-1,) + (1,) * (len(shape) - 1 - dim))
    return factor_of


def noise(own_key, extent, spread, reach, shards=(), kind=jnp.bfloat16):
    loudness = level_of(own_key, extent, shards, -0.22, 0.18) if shards else 1.0
    array = jax.random.normal(own_key, extent, jnp.float32) * spread * loudness
    return jnp.minimum(jnp.maximum(array, -reach), reach).astype(kind)


def setup_inputs(seed: int = 0) -> dict:
    keys = jax.random.split(jax.random.key(seed), 6)
    return {
        "image_embed": noise(keys[0], (TOKENS, D), 0.03125, 0.25, ((0, 768),)),
        "text_embed": noise(keys[1], (TOKENS, D), 0.03125, 0.25, ((0, 768),)),
        "positive_partner_index": draw_positive_partner_index(jax.random.fold_in(keys[5], 71), 0),
        "exponent_of_multiplier": jnp.clip(jax.random.uniform(keys[3], (1,), jnp.float32, 1.0, 2.0), 1.0, 2.0),
        "logit_bias": jnp.clip(jax.random.uniform(keys[4], (1,), jnp.float32, -4.0, -1.0), -4.0, -1.0),
    }


def normalize(values):
    wide = values.astype(jnp.float32)
    norms = jnp.sqrt(lax.optimization_barrier(jnp.sum(wide * wide, axis=-1, keepdims=True)) + 1e-06)
    return (wide / norms, norms)

def back_through(unit, norms, grad):
    return (grad - unit * lax.optimization_barrier(jnp.sum(unit * grad, axis=-1, keepdims=True))) / norms

def evaluate_tile_affinities(leading_unitlength, latter_unitlength, matching_entry_position, leading_field_position, affinity_multiplier, trainable_offset_term):
    affinity_matrix = affinity_multiplier * lax.dot_general(leading_unitlength, latter_unitlength, (((1,), (1,)), ((), ())), preferred_element_type=jnp.float32) + trainable_offset_term
    columns = leading_field_position + jnp.arange(latter_unitlength.shape[0]).astype(jnp.int32)
    labels = jnp.where(matching_entry_position[:, None] == columns[None, :], 1.0, -1.0).astype(jnp.float32)
    target_polarity = (-labels * jax.nn.sigmoid(-labels * affinity_matrix)).astype(jnp.bfloat16)
    leading_piece = affinity_multiplier * jnp.dot(target_polarity, latter_unitlength, preferred_element_type=jnp.float32)
    latter_piece = affinity_multiplier * lax.dot_general(target_polarity, leading_unitlength, (((0,), (0,)), ((), ())), preferred_element_type=jnp.float32)
    return (leading_piece, latter_piece)

def reference(image_embed, text_embed, positive_partner_index, exponent_of_multiplier, logit_bias):
    affinity_multiplier = jnp.exp(exponent_of_multiplier[0])
    trainable_offset_term = logit_bias[0]
    leading_unitlength, image_norm = normalize(image_embed)
    latter_unitlength, text_norm = normalize(text_embed)
    leading_cyclic_offset = leading_unitlength.astype(jnp.bfloat16).reshape(GROUPS, CYCLE, ROWS, D)
    latter_cyclic_offset = latter_unitlength.astype(jnp.bfloat16).reshape(GROUPS, CYCLE, ROWS, D)
    blocks = GROUPS * CYCLE
    pair_blocks = positive_partner_index.reshape(blocks, ROWS)
    group_idx = jnp.broadcast_to(jnp.arange(GROUPS).astype(jnp.int32)[:, None], (GROUPS, CYCLE))
    cycle_idx = jnp.broadcast_to(jnp.arange(CYCLE).astype(jnp.int32)[None, :], (GROUPS, CYCLE))
    plans = [(latter_cyclic_offset, group_idx, cycle_idx), (jnp.roll(latter_cyclic_offset, 1, axis=1), group_idx, (cycle_idx + CYCLE - 1) % CYCLE), (jnp.roll(latter_cyclic_offset, 2, axis=1), group_idx, (cycle_idx + CYCLE - 2) % CYCLE), (jnp.roll(latter_cyclic_offset, 1, axis=0), (group_idx + GROUPS - 1) % GROUPS, cycle_idx)]
    image_flat = leading_cyclic_offset.reshape(blocks, ROWS, D)
    normalized_first_gradient = jnp.zeros((blocks, ROWS, D), jnp.float32)
    parts = []
    for texts, text_group, text_cycle in plans:
        firsts = ((text_group * CYCLE + text_cycle) * ROWS).reshape(blocks).astype(jnp.int32)

        def one_block(phrase_total):
            return evaluate_tile_affinities(phrase_total[0], phrase_total[1], phrase_total[2], phrase_total[3], affinity_multiplier, trainable_offset_term)
        leading_piece, latter_piece = lax.map(one_block, (image_flat, texts.reshape(blocks, ROWS, D), pair_blocks, firsts))
        normalized_first_gradient = normalized_first_gradient + leading_piece
        parts.append(latter_piece.reshape(GROUPS, CYCLE, ROWS, D))
    unit_text_grad = parts[0] + jnp.roll(parts[1], -1, axis=1) + jnp.roll(parts[2], -2, axis=1) + jnp.roll(parts[3], -1, axis=0)
    image_grad = back_through(leading_unitlength, image_norm, normalized_first_gradient.reshape(TOKENS, D))
    text_grad = back_through(latter_unitlength, text_norm, unit_text_grad.reshape(TOKENS, D))
    return (image_grad, text_grad)
```

```python
import jax
import jax.numpy as jnp
from jax import lax
from jax.sharding import PartitionSpec as P

CODE_ROWS = 16
NO_MATCH = -256.0


def from_behind(array, axis, by):
    count = lax.axis_size(axis)
    return lax.ppermute(array, axis, [(i, (i + by) % count) for i in range(count)])


def normalize(values):
    wide = values.astype(jnp.float32)
    norms = jnp.sqrt(jnp.sum(wide * wide, axis=-1, keepdims=True) + 1e-06)
    return (wide / norms, norms)


def rounded(values):
    return normalize(values)[0].astype(jnp.bfloat16)


def back_through(unit, norms, grad):
    return (grad - unit * jnp.sum(unit * grad, axis=-1, keepdims=True)) / norms


def scores_of(rows, columns, multiplier, bias):
    return (
        multiplier
        * lax.dot_general(
            rows, columns, (((1,), (1,)), ((), ())), preferred_element_type=jnp.float32
        )
        + bias
    )


def signal_of(scores, matches):
    labels = jnp.where(matches, 1.0, -1.0).astype(jnp.float32)
    return (-labels * jax.nn.sigmoid(-labels * scores)).astype(jnp.bfloat16)


def dot(a, b):
    return jnp.dot(a, b, preferred_element_type=jnp.float32)


def per_device(image_embed, text_embed, partner, exponent_of_multiplier, logit_bias):
    multiplier = jnp.exp(exponent_of_multiplier[0])
    bias = logit_bias[0]
    cycle = lax.axis_size("blk")
    groups = lax.axis_size("group")
    rows, width = image_embed.shape
    g = lax.axis_index("group")
    b = lax.axis_index("blk")

    def first_of(group_at, cycle_at):
        return (group_at * cycle + cycle_at) * rows

    links = [
        ("blk", 1, first_of(g, (b + cycle - 1) % cycle)),
        ("group", 1, first_of((g + groups - 1) % groups, b)),
        ("blk", 2, first_of(g, (b + cycle - 2) % cycle)),
    ]
    text_in = [from_behind(text_embed, axis, by) for axis, by, _ in links]
    near_image = from_behind(image_embed, "blk", -1)
    near_partner = from_behind(partner, "blk", -1)

    image_unit, image_norm = normalize(image_embed)
    image_round = image_unit.astype(jnp.bfloat16)

    def code_of(partners, text_first):
        place = partners - text_first
        inside = (place >= 0) & (place < rows)
        return jnp.where(inside, (place - rows // 2).astype(jnp.float32), NO_MATCH)

    codes = jnp.stack([code_of(partner, first) for _, _, first in links])
    codes = jnp.pad(codes, ((0, CODE_ROWS - len(links)), (0, width - rows)))
    packed = jnp.concatenate([image_round, codes.astype(jnp.bfloat16)])
    packed, text_in[1], text_in[2] = lax.optimization_barrier((packed, text_in[1], text_in[2]))
    packed_in = [None] + [from_behind(packed, axis, -by) for axis, by, _ in links[1:]]

    text_unit, text_norm = normalize(text_embed)
    text_round = text_unit.astype(jnp.bfloat16)

    columns = jnp.arange(rows, dtype=jnp.int32)

    def forward(text, text_first):
        matches = partner[:, None] == (text_first + columns)[None, :]
        return signal_of(scores_of(image_round, text, multiplier, bias), matches)

    def backward(image, code):
        matches = code[None, :] == (columns - rows // 2).astype(jnp.float32)[:, None]
        return signal_of(scores_of(text_round, image, multiplier, bias), matches)

    own = forward(text_round, first_of(g, b))
    image_sum = dot(own, text_round)
    text_sum = lax.dot_general(
        own, image_round, (((0,), (0,)), ((), ())), preferred_element_type=jnp.float32
    )
    for i in (2, 1, 0):
        text = rounded(text_in[i])
        image_sum = image_sum + dot(forward(text, links[i][2]), text)
        if i > 0:
            image = packed_in[i][:rows]
            code = packed_in[i][rows + i, :rows].astype(jnp.float32)
        else:
            image = rounded(near_image)
            code = code_of(near_partner, first_of(g, b))
        text_sum = text_sum + dot(backward(image, code), image)
    image_grad = back_through(image_unit, image_norm, multiplier * image_sum)
    text_grad = back_through(text_unit, text_norm, multiplier * text_sum)
    return (image_grad, text_grad)


def solution(mesh):
    return jax.shard_map(
        per_device,
        mesh=mesh,
        in_specs=(
            P(("group", "blk"), None),
            P(("group", "blk"), None),
            P(("group", "blk")),
            P(),
            P(),
        ),
        out_specs=(P(("group", "blk"), None), P(("group", "blk"), None)),
        check_vma=False,
    )
```

```python
import functools

import jax
import jax.numpy as jnp
from jax import lax
from jax.experimental import pallas as pl
from jax.experimental.pallas import tpu as pltpu
from jax.sharding import PartitionSpec as P

CODE_ROWS = 16
NO_MATCH = -256.0
VMEM_LIMIT = 32 * 1024 * 1024
LAST_ROWS = 128
BLK_1, GROUP_1, BLK_2, OWN = range(4)


def units_of(values):
    wide = values.astype(jnp.float32)
    scale = lax.rsqrt(jnp.sum(wide * wide, axis=-1, keepdims=True) + 1e-06)
    return wide * scale, scale


def write_codes(ints, partner_ref, out_ref):
    rows, width = partner_ref.shape[0], out_ref.shape[1]
    partner = partner_ref[...].reshape(1, rows)
    row = lax.broadcasted_iota(jnp.int32, (CODE_ROWS, rows), 0)
    codes = jnp.full((CODE_ROWS, rows), NO_MATCH, jnp.float32)
    for kind in range(4):
        place = partner - ints[kind]
        inside = (place >= 0) & (place < rows)
        code = jnp.where(inside, (place - rows // 2).astype(jnp.float32), NO_MATCH)
        codes = jnp.where(row == kind, code, codes)
    out_ref[rows:, :rows] = codes.astype(out_ref.dtype)
    out_ref[rows:, rows:] = jnp.zeros((CODE_ROWS, width - rows), out_ref.dtype)


def first_kernel(ints, image_ref, text_ref, partner_ref, out_ref, done):
    rows = image_ref.shape[0]

    def bring(ref):
        copy = pltpu.make_async_copy(ref, out_ref.at[:rows, :], done)
        copy.start()
        copy.wait()

    pl.when(ints[4] != 0)(lambda: bring(image_ref))
    pl.when(ints[4] == 0)(lambda: bring(text_ref))
    write_codes(ints, partner_ref, out_ref)


def second_kernel(ints, image_ref, text_ref, partner_ref, packed_ref, out_ref):
    rows = image_ref.shape[0]
    packed_ref[:rows, :] = units_of(image_ref[...])[0].astype(packed_ref.dtype)
    write_codes(ints, partner_ref, packed_ref)

    @pl.when(ints[4] == 0)
    def _():
        out_ref[...] = packed_ref[...]

    @pl.when(ints[4] != 0)
    def _():
        out_ref[:rows, :] = text_ref[...]
        out_ref[rows:, :] = jnp.zeros((CODE_ROWS, text_ref.shape[1]), out_ref.dtype)


def pack(kernel, outs, ints, image, text, partner, copies=False):
    rows, width = image.shape
    vmem = pl.BlockSpec(memory_space=pltpu.VMEM)
    given = pl.BlockSpec(memory_space=pl.ANY) if copies else vmem
    return pl.pallas_call(
        kernel,
        out_shape=[jax.ShapeDtypeStruct((rows + CODE_ROWS, width), jnp.bfloat16)] * outs,
        in_specs=[pl.BlockSpec(memory_space=pltpu.SMEM), given, given, vmem],
        out_specs=[vmem] * outs,
        scratch_shapes=[pltpu.SemaphoreType.DMA] if copies else [],
        compiler_params=pltpu.CompilerParams(vmem_limit_bytes=VMEM_LIMIT),
        cost_estimate=pl.CostEstimate(
            flops=4 * rows * width, bytes_accessed=4 * rows * width, transcendentals=rows
        ),
    )(ints, image, text, partner)


def term(side, kind, ints, floats, unit, foreign_ref, other, partner_ref):
    rows = unit.shape[0]
    block = foreign_ref[...]
    if other is not None:
        other_ref, taken = other
        block = jnp.where(ints[taken] != 0, other_ref[: block.shape[0], :], block)
    if side == "image":
        foreign = units_of(block[:rows, :])[0].astype(jnp.bfloat16)
    elif other is not None:
        foreign = jnp.where(
            ints[taken] != 0, units_of(block[:rows, :])[0].astype(jnp.bfloat16), block[:rows, :]
        )
    else:
        foreign = block[:rows, :]
    scores = (
        floats[0]
        * lax.dot_general(
            unit.astype(jnp.bfloat16),
            foreign,
            (((1,), (1,)), ((), ())),
            preferred_element_type=jnp.float32,
        )
        + floats[1]
    )
    if side == "image":
        columns = ints[kind] + lax.broadcasted_iota(jnp.int32, scores.shape, 1)
        matches = partner_ref[...] == columns
    else:
        code = block[rows:, :rows].astype(jnp.float32)[kind : kind + 1, :]
        place = lax.broadcasted_iota(jnp.int32, scores.shape, 0) - rows // 2
        matches = place.astype(jnp.float32) == code
    slope = jax.nn.sigmoid(jnp.where(matches, -scores, scores))
    signal = jnp.where(matches, -slope, slope).astype(jnp.bfloat16)
    return jnp.dot(signal, foreign, preferred_element_type=jnp.float32)


def sum_kernel(plan, last, ints, floats, *refs):
    refs = list(refs)
    partner_ref = refs.pop(0)
    copies = []
    if last:
        done = refs.pop()
        held_refs = [refs.pop() for _ in plan]
    out_refs = refs[-len(plan) :]
    for at, ((side, continues, kinds), out_ref) in enumerate(zip(plan, out_refs)):
        own_ref = refs.pop(0)
        unit, scale = units_of(own_ref[...])
        total = refs.pop(0)[...] if continues else None
        for kind, taken in kinds:
            foreign_ref = refs.pop(0)
            other = None if taken is None else (refs.pop(0), taken)
            more = term(side, kind, ints, floats, unit, foreign_ref, other, partner_ref)
            total = more if total is None else total + more
        if not last:
            out_ref[...] = total
            continue
        held = held_refs[at]
        for n, start in enumerate(range(0, total.shape[0], LAST_ROWS)):
            here = slice(start, start + LAST_ROWS)
            part = floats[0] * total[here]
            along = jnp.sum(unit[here] * part, axis=-1, keepdims=True)
            held[here, :] = (part - unit[here] * along) * scale[here]
            copy = pltpu.make_async_copy(held.at[here, :], out_ref.at[here, :], done.at[at, n])
            copy.start()
            copies.append(copy)
    for copy in copies:
        copy.wait()


def sums(ints, floats, partner, own, work, last=False):
    plan, args = [], [partner]
    for side, (so_far, links) in work.items():
        plan.append((side, so_far is not None, tuple((k, i if o is not None else None) for k, _, o, i in links)))
        args.append(own[side])
        if so_far is not None:
            args.append(so_far)
        for _, block, other, _ in links:
            args += [block] if other is None else [block, other]
    rows, width = own["image"].shape
    terms = sum(len(links) for _, links in work.values())
    vmem = pl.BlockSpec(memory_space=pltpu.VMEM)
    return pl.pallas_call(
        functools.partial(sum_kernel, tuple(plan), last),
        out_shape=[jax.ShapeDtypeStruct((rows, width), jnp.float32)] * len(plan),
        in_specs=[pl.BlockSpec(memory_space=pltpu.SMEM)] * 2 + [vmem] * len(args),
        out_specs=[pl.BlockSpec(memory_space=pl.ANY) if last else vmem] * len(plan),
        scratch_shapes=[pltpu.VMEM((rows, width), jnp.float32)] * len(plan)
        + [pltpu.SemaphoreType.DMA((len(plan), rows // LAST_ROWS))]
        if last
        else [],
        compiler_params=pltpu.CompilerParams(vmem_limit_bytes=VMEM_LIMIT),
        cost_estimate=pl.CostEstimate(
            flops=4 * terms * rows * rows * width,
            bytes_accessed=12 * terms * rows * width,
            transcendentals=terms * rows * rows,
        ),
    )(ints, floats, *args)


def per_device(image_embed, text_embed, partner, exponent_of_multiplier, logit_bias):
    floats = jnp.concatenate([jnp.exp(exponent_of_multiplier), logit_bias])
    cycle = lax.axis_size("blk")
    groups = lax.axis_size("group")
    rows = image_embed.shape[0]
    g = lax.axis_index("group")
    b = lax.axis_index("blk")

    def send(array, target):
        pairs = []
        for i in range(groups):
            for j in range(cycle):
                to = target(i, j)
                if to is not None:
                    pairs.append((i * cycle + j, (to[0] % groups) * cycle + to[1] % cycle))
        return lax.ppermute(array, ("group", "blk"), pairs)

    def first_of(group_at, cycle_at):
        return (group_at * cycle + cycle_at) * rows

    text_first = [
        first_of(g, (b + cycle - 1) % cycle),
        first_of((g + groups - 1) % groups, b),
        first_of(g, (b + cycle - 2) % cycle),
        first_of(g, b),
    ]
    ints = jnp.stack(text_first + [jnp.int32(g == 0), jnp.int32(g == groups - 1)])
    is_first, is_last = 4, 5
    partner_column = partner[:, None]

    (early,) = pack(first_kernel, 1, ints, image_embed, text_embed, partner, copies=True)
    early, image_again, text_again = lax.optimization_barrier((early, image_embed, text_embed))
    early_in = send(early, lambda i, j: (i, j - 1) if i == 0 else (i, j + 1))
    packed, late = pack(second_kernel, 2, ints, image_again, text_embed, partner)
    x_text = send(text_again, lambda i, j: (i, j + 2))
    x_image = send(packed, lambda i, j: (i, j - 2))
    late_in = send(late, lambda i, j: (i, j + 1) if i == 0 else (i, j - 1))
    packed, text_again = lax.optimization_barrier((packed, text_again))
    group_text = send(text_again, lambda i, j: (i + 1, j) if i < groups - 1 else None)
    handed = send(
        early_in,
        lambda i, j: (groups - 1, j + 1) if i == 0 else (0, j - 1) if i == groups - 1 else None,
    )
    packed_again, early_in = lax.optimization_barrier((packed, early_in))
    group_image = send(packed_again, lambda i, j: (i - 1, j) if i > 0 else None)

    step = functools.partial(sums, ints, floats, partner_column, {"image": image_embed, "text": text_embed})
    image_sum, text_sum = step({
        "image": (None, [(OWN, text_embed, None, None), (BLK_2, x_text, None, None)]),
        "text": (None, [(OWN, packed, None, None), (BLK_2, x_image, None, None)]),
    })
    image_sum, text_sum = step({
        "image": (image_sum, [(BLK_1, early_in, late_in, is_first)]),
        "text": (text_sum, [(BLK_1, late_in, early_in, is_first)]),
    })
    return step({
        "image": (image_sum, [(GROUP_1, group_text, handed, is_first)]),
        "text": (text_sum, [(GROUP_1, group_image, handed, is_last)]),
    }, last=True)


def solution(mesh):
    return jax.shard_map(
        per_device,
        mesh=mesh,
        in_specs=(
            P(("group", "blk"), None),
            P(("group", "blk"), None),
            P(("group", "blk")),
            P(),
            P(),
        ),
        out_specs=(P(("group", "blk"), None), P(("group", "blk"), None)),
        check_vma=False,
    )
```

```python
import functools

import jax
import jax.numpy as jnp
from jax import lax
from jax.experimental import pallas as pl
from jax.experimental.pallas import tpu as pltpu
from jax.sharding import PartitionSpec as P

CODE_ROWS = 8
NO_MATCH = -256.0
VMEM_LIMIT = 32 * 1024 * 1024
LAST_ROWS = 64
BLK_1, GROUP_1, BLK_2, OWN = range(4)


def units_of(values):
    wide = values.astype(jnp.float32)
    scale = lax.rsqrt(jnp.sum(wide * wide, axis=-1, keepdims=True) + 1e-06)
    return wide * scale, scale


def codes_of(ints, partner):
    rows = partner.shape[1]
    row = lax.broadcasted_iota(jnp.int32, (CODE_ROWS, rows), 0)
    codes = jnp.full((CODE_ROWS, rows), NO_MATCH, jnp.float32)
    for kind in range(4):
        place = partner - ints[kind]
        inside = (place >= 0) & (place < rows)
        code = jnp.where(inside, (place - rows // 2).astype(jnp.float32), NO_MATCH)
        codes = jnp.where(row == kind, code, codes)
    return codes


def pack_kernel(flags, ints, image_ref, text_ref, partner_ref, *refs):
    out_refs, done = refs[:-1], refs[-1]
    rows, width = image_ref.shape
    for n, (flag, out_ref) in enumerate(zip(flags, out_refs)):

        def begin(ref, n=n, out_ref=out_ref):
            pltpu.make_async_copy(ref, out_ref.at[:rows, :], done.at[n]).start()

        if flag is None:
            begin(image_ref)
        else:
            pl.when(ints[flag] != 0)(lambda begin=begin: begin(image_ref))
            pl.when(ints[flag] == 0)(lambda begin=begin: begin(text_ref))
    codes = codes_of(ints, partner_ref[...].reshape(1, rows))
    for out_ref in out_refs:
        out_ref[rows:, :rows] = codes.astype(out_ref.dtype)
        out_ref[rows:, rows:] = jnp.zeros((CODE_ROWS, width - rows), out_ref.dtype)
    for n, out_ref in enumerate(out_refs):
        pltpu.make_async_copy(image_ref, out_ref.at[:rows, :], done.at[n]).wait()


def pack(flags, ints, image, text, partner):
    rows, width = image.shape
    vmem, given = pl.BlockSpec(memory_space=pltpu.VMEM), pl.BlockSpec(memory_space=pl.ANY)
    return pl.pallas_call(
        functools.partial(pack_kernel, flags),
        out_shape=[jax.ShapeDtypeStruct((rows + CODE_ROWS, width), jnp.bfloat16)] * len(flags),
        in_specs=[pl.BlockSpec(memory_space=pltpu.SMEM), given, given, vmem],
        out_specs=[vmem] * len(flags),
        scratch_shapes=[pltpu.SemaphoreType.DMA((len(flags),))],
        compiler_params=pltpu.CompilerParams(vmem_limit_bytes=VMEM_LIMIT),
        cost_estimate=pl.CostEstimate(
            flops=rows * width, bytes_accessed=4 * len(flags) * rows * width, transcendentals=0
        ),
    )(ints, image, text, partner)


def term(side, kind, ints, floats, unit, foreign_refs, picks, partner_ref):
    rows = unit.shape[0]
    block = foreign_refs[0][...]
    for other_ref, flag in zip(foreign_refs[1:], picks):
        block = jnp.where(ints[flag] != 0, other_ref[...], block)
    foreign = units_of(block[:rows, :])[0].astype(jnp.bfloat16)
    scores = (
        floats[0]
        * lax.dot_general(
            unit.astype(jnp.bfloat16),
            foreign,
            (((1,), (1,)), ((), ())),
            preferred_element_type=jnp.float32,
        )
        + floats[1]
    )
    if side == "image":
        columns = ints[kind] + lax.broadcasted_iota(jnp.int32, scores.shape, 1)
        matches = partner_ref[...] == columns
    else:
        code = block[rows:, :rows].astype(jnp.float32)[kind : kind + 1, :]
        place = lax.broadcasted_iota(jnp.int32, scores.shape, 0) - rows // 2
        matches = place.astype(jnp.float32) == code
    slope = jax.nn.sigmoid(jnp.where(matches, -scores, scores))
    signal = jnp.where(matches, -slope, slope).astype(jnp.bfloat16)
    return jnp.dot(signal, foreign, preferred_element_type=jnp.float32)


def finish(floats, own_ref, sum_ref, held, out_ref, done):
    copies = []
    for n, start in enumerate(range(0, own_ref.shape[0], LAST_ROWS)):
        here = slice(start, start + LAST_ROWS)
        unit, scale = units_of(own_ref[here, :])
        part = floats[0] * sum_ref[here, :]
        along = jnp.sum(unit * part, axis=-1, keepdims=True)
        held[here, :] = (part - unit * along) * scale
        copies.append(pltpu.make_async_copy(held.at[here, :], out_ref.at[here, :], done.at[n]))
        copies[-1].start()
    for copy in copies:
        copy.wait()


def early_kernel(odd, ints, floats, image, text, partner, packed, x_text, x_image, chip, image_sum, text_sum):
    image_unit, text_unit = units_of(image[...])[0], units_of(text[...])[0]
    image_sum[...] = term("image", OWN, ints, floats, image_unit, [text], (), partner)
    image_sum[...] += term("image", BLK_2, ints, floats, image_unit, [x_text], (), partner)
    text_sum[...] = term("text", OWN, ints, floats, text_unit, [packed], (), partner)
    text_sum[...] += term("text", BLK_2, ints, floats, text_unit, [x_image], (), partner)

    @pl.when(ints[odd] != 0)
    def _():
        image_sum[...] += term("image", GROUP_1, ints, floats, image_unit, [chip], (), partner)

    @pl.when(ints[odd] == 0)
    def _():
        text_sum[...] += term("text", GROUP_1, ints, floats, text_unit, [chip], (), partner)


def middle_kernel(
    odd, first, ints, floats, image, text, partner, image_so_far, text_so_far, early, late,
    image_sum, text_sum, image_grad, text_grad, held, done,
):
    image_unit, text_unit = units_of(image[...])[0], units_of(text[...])[0]

    def image_term():
        more = term("image", BLK_1, ints, floats, image_unit, [early, late], (first,), partner)
        image_sum[...] = image_so_far[...] + more

    def text_term():
        more = term("text", BLK_1, ints, floats, text_unit, [late, early], (first,), partner)
        text_sum[...] = text_so_far[...] + more

    image_term()
    text_term()

    @pl.when(ints[odd] != 0)
    def _():
        finish(floats, image, image_sum, held, image_grad, done)

    @pl.when(ints[odd] == 0)
    def _():
        finish(floats, text, text_sum, held, text_grad, done)


def last_kernel(
    odd, first, final, ints, floats, image, text, partner, image_so_far, text_so_far, link, handed,
    image_done, text_done, image_grad, text_grad, total, held, done,
):
    @pl.when(ints[odd] != 0)
    def _():
        unit = units_of(text[...])[0]
        more = term("text", GROUP_1, ints, floats, unit, [link, handed], (final,), partner)
        total[...] = text_so_far[...] + more
        finish(floats, text, total, held, text_grad, done)

    @pl.when(ints[odd] == 0)
    def _():
        unit = units_of(image[...])[0]
        more = term("image", GROUP_1, ints, floats, unit, [link, handed], (first,), partner)
        total[...] = image_so_far[...] + more
        finish(floats, image, total, held, image_grad, done)


def call(kernel, terms, sums, grads, held, ints, floats, *args, aliased=0):
    rows, width = args[0].shape
    vmem, given = pl.BlockSpec(memory_space=pltpu.VMEM), pl.BlockSpec(memory_space=pl.ANY)
    shape = jax.ShapeDtypeStruct((rows, width), jnp.float32)
    plain = len(args) - aliased
    return pl.pallas_call(
        kernel,
        out_shape=[shape] * (sums + grads),
        in_specs=[pl.BlockSpec(memory_space=pltpu.SMEM)] * 2 + [vmem] * plain + [given] * aliased,
        out_specs=[vmem] * sums + [given] * grads,
        input_output_aliases={2 + plain + n: n for n in range(aliased)},
        scratch_shapes=[pltpu.VMEM((rows, width), jnp.float32)] * held
        + ([pltpu.SemaphoreType.DMA((rows // LAST_ROWS,))] if held else []),
        compiler_params=pltpu.CompilerParams(vmem_limit_bytes=VMEM_LIMIT),
        cost_estimate=pl.CostEstimate(
            flops=4 * terms * rows * rows * width,
            bytes_accessed=12 * terms * rows * width,
            transcendentals=terms * rows * rows,
        ),
    )(ints, floats, *args)


def per_device(image_embed, text_embed, partner, exponent_of_multiplier, logit_bias):
    floats = jnp.concatenate([jnp.exp(exponent_of_multiplier), logit_bias])
    cycle = lax.axis_size("blk")
    groups = lax.axis_size("group")
    rows = image_embed.shape[0]
    g = lax.axis_index("group")
    b = lax.axis_index("blk")

    def send(array, target):
        pairs = []
        for i in range(groups):
            for j in range(cycle):
                to = target(i, j)
                if to is not None:
                    pairs.append((i * cycle + j, (to[0] % groups) * cycle + to[1] % cycle))
        return lax.ppermute(array, ("group", "blk"), pairs)

    def first_of(group_at, cycle_at):
        return (group_at * cycle + cycle_at) * rows

    text_first = [
        first_of(g, (b + cycle - 1) % cycle),
        first_of((g + groups - 1) % groups, b),
        first_of(g, (b + cycle - 2) % cycle),
        first_of(g, b),
    ]
    is_first_group = g == 0
    flags = [is_first_group, g != 0, g % 2 == 1, g % 2 == 0, g == groups - 1]
    ints = jnp.stack(text_first + [flag.astype(jnp.int32) for flag in flags])
    is_first, not_first, is_odd, is_even, is_last = range(4, 9)

    codes = codes_of(text_first, partner[None, :])
    codes = jnp.pad(codes.astype(jnp.bfloat16), ((0, 0), (0, image_embed.shape[1] - rows)))
    early = jnp.concatenate([jnp.where(is_first_group, image_embed, text_embed), codes])
    early, image_again, text_again = lax.optimization_barrier((early, image_embed, text_embed))
    early_in = send(early, lambda i, j: (i, j - 1) if i == 0 else (i, j + 1))
    late, link, chip, packed = pack(
        (not_first, is_even, is_odd, None), ints, image_again, text_again, partner
    )
    x_text = send(text_again, lambda i, j: (i, j + 2))
    x_image = send(packed, lambda i, j: (i, j - 2))
    late_in = send(late, lambda i, j: (i, j + 1) if i == 0 else (i, j - 1))
    link, early_in = lax.optimization_barrier((link, early_in))
    chip_in = send(chip, lambda i, j: (i ^ 1, j))
    link_in = send(
        link, lambda i, j: None if i in (0, groups - 1) else (i + 1, j) if i % 2 else (i - 1, j)
    )
    handed = send(
        early_in,
        lambda i, j: (groups - 1, j + 1) if i == 0 else (0, j - 1) if i == groups - 1 else None,
    )

    own = (image_embed, text_embed, partner[:, None])
    kernel = functools.partial(early_kernel, is_odd)
    so_far = call(kernel, 5, 2, 0, 0, ints, floats, *own, packed, x_text, x_image, chip_in)
    kernel = functools.partial(middle_kernel, is_odd, is_first)
    *so_far, image_grad, text_grad = call(
        kernel, 2, 2, 2, 1, ints, floats, *own, *so_far, early_in, late_in
    )
    kernel = functools.partial(last_kernel, is_odd, is_first, is_last)
    return call(
        kernel, 1, 0, 2, 2, ints, floats, *own, *so_far, link_in, handed, image_grad, text_grad, aliased=2
    )


def solution(mesh):
    return jax.shard_map(
        per_device,
        mesh=mesh,
        in_specs=(
            P(("group", "blk"), None),
            P(("group", "blk"), None),
            P(("group", "blk")),
            P(),
            P(),
        ),
        out_specs=(P(("group", "blk"), None), P(("group", "blk"), None)),
        check_vma=False,
    )
```

```python
import functools

import jax
import jax.numpy as jnp
from jax import lax
from jax.experimental import pallas as pl
from jax.experimental.pallas import tpu as pltpu
from jax.sharding import PartitionSpec as P

CODE_ROWS = 8
NO_MATCH = -256.0
VMEM_LIMIT = 32 * 1024 * 1024
LAST_ROWS = 64
BLK_1, GROUP_1, BLK_2, OWN = range(4)


def units_of(values):
    wide = values.astype(jnp.float32)
    scale = lax.rsqrt(jnp.sum(wide * wide, axis=-1, keepdims=True) + 1e-06)
    return wide * scale, scale


def codes_of(ints, partner):
    rows = partner.shape[1]
    row = lax.broadcasted_iota(jnp.int32, (CODE_ROWS, rows), 0)
    codes = jnp.full((CODE_ROWS, rows), NO_MATCH, jnp.float32)
    for kind in range(4):
        place = partner - ints[kind]
        inside = (place >= 0) & (place < rows)
        code = jnp.where(inside, (place - rows // 2).astype(jnp.float32), NO_MATCH)
        codes = jnp.where(row == kind, code, codes)
    return codes


def pack_kernel(flags, ints, image_ref, text_ref, partner_ref, *refs):
    out_refs, done = refs[:-1], refs[-1]
    rows, width = image_ref.shape
    for n, (flag, out_ref) in enumerate(zip(flags, out_refs)):

        def begin(ref, n=n, out_ref=out_ref):
            pltpu.make_async_copy(ref, out_ref.at[:rows, :], done.at[n]).start()

        if flag is None:
            begin(image_ref)
        else:
            pl.when(ints[flag] != 0)(lambda begin=begin: begin(image_ref))
            pl.when(ints[flag] == 0)(lambda begin=begin: begin(text_ref))
    codes = codes_of(ints, partner_ref[...].reshape(1, rows))
    for out_ref in out_refs:
        out_ref[rows:, :rows] = codes.astype(out_ref.dtype)
        out_ref[rows:, rows:] = jnp.zeros((CODE_ROWS, width - rows), out_ref.dtype)
    for n, out_ref in enumerate(out_refs):
        pltpu.make_async_copy(image_ref, out_ref.at[:rows, :], done.at[n]).wait()


def pack(flags, ints, image, text, partner):
    rows, width = image.shape
    vmem, given = pl.BlockSpec(memory_space=pltpu.VMEM), pl.BlockSpec(memory_space=pl.ANY)
    return pl.pallas_call(
        functools.partial(pack_kernel, flags),
        out_shape=[jax.ShapeDtypeStruct((rows + CODE_ROWS, width), jnp.bfloat16)] * len(flags),
        in_specs=[pl.BlockSpec(memory_space=pltpu.SMEM), given, given, vmem],
        out_specs=[vmem] * len(flags),
        scratch_shapes=[pltpu.SemaphoreType.DMA((len(flags),))],
        compiler_params=pltpu.CompilerParams(vmem_limit_bytes=VMEM_LIMIT),
        cost_estimate=pl.CostEstimate(
            flops=rows * width, bytes_accessed=4 * len(flags) * rows * width, transcendentals=0
        ),
    )(ints, image, text, partner)


def term(side, kind, ints, floats, unit, foreign_refs, picks, partner_ref):
    rows = unit.shape[0]
    height = rows if side == "image" else rows + CODE_ROWS
    block = foreign_refs[0][:height, :]
    for other_ref, flag in zip(foreign_refs[1:], picks):
        block = jnp.where(ints[flag] != 0, other_ref[:height, :], block)
    foreign = units_of(block[:rows, :])[0].astype(jnp.bfloat16)
    scores = (
        floats[0]
        * lax.dot_general(
            unit.astype(jnp.bfloat16),
            foreign,
            (((1,), (1,)), ((), ())),
            preferred_element_type=jnp.float32,
        )
        + floats[1]
    )
    if side == "image":
        columns = ints[kind] + lax.broadcasted_iota(jnp.int32, scores.shape, 1)
        matches = partner_ref[...] == columns
    else:
        code = block[rows:, :rows].astype(jnp.float32)[kind : kind + 1, :]
        place = lax.broadcasted_iota(jnp.int32, scores.shape, 0) - rows // 2
        matches = place.astype(jnp.float32) == code
    slope = jax.nn.sigmoid(jnp.where(matches, -scores, scores))
    signal = jnp.where(matches, -slope, slope).astype(jnp.bfloat16)
    return jnp.dot(signal, foreign, preferred_element_type=jnp.float32)


def finish(floats, own_ref, sum_ref, held, out_ref, done):
    copies = []
    for n, start in enumerate(range(0, own_ref.shape[0], LAST_ROWS)):
        here = slice(start, start + LAST_ROWS)
        unit, scale = units_of(own_ref[here, :])
        part = floats[0] * sum_ref[here, :]
        along = jnp.sum(unit * part, axis=-1, keepdims=True)
        held[here, :] = (part - unit * along) * scale
        copies.append(pltpu.make_async_copy(held.at[here, :], out_ref.at[here, :], done.at[n]))
        copies[-1].start()
    for copy in copies:
        copy.wait()


def own_kernel(ints, floats, image, text, partner, packed, image_sum, text_sum):
    image_unit, text_unit = units_of(image[...])[0], units_of(text[...])[0]
    image_sum[...] = term("image", OWN, ints, floats, image_unit, [text], (), partner)
    text_sum[...] = term("text", OWN, ints, floats, text_unit, [packed], (), partner)


def x_kernel(
    ints, floats, image, text, partner, image_so_far, text_so_far, x_text, x_image, image_sum, text_sum
):
    image_unit, text_unit = units_of(image[...])[0], units_of(text[...])[0]
    more = term("image", BLK_2, ints, floats, image_unit, [x_text], (), partner)
    image_sum[...] = image_so_far[...] + more
    more = term("text", BLK_2, ints, floats, text_unit, [x_image], (), partner)
    text_sum[...] = text_so_far[...] + more


def middle_kernel(
    odd, first, ints, floats, image, text, partner, image_so_far, text_so_far, early_text, early_image, late, chip,
    image_sum, text_sum, image_grad, text_grad, held, done,
):
    image_unit, text_unit = units_of(image[...])[0], units_of(text[...])[0]
    more = term("image", BLK_1, ints, floats, image_unit, [early_text, late], (first,), partner)
    image_sum[...] = image_so_far[...] + more
    more = term("text", BLK_1, ints, floats, text_unit, [late, early_image], (first,), partner)
    text_sum[...] = text_so_far[...] + more

    @pl.when(ints[odd] != 0)
    def _():
        image_sum[...] += term("image", GROUP_1, ints, floats, image_unit, [chip], (), partner)
        finish(floats, image, image_sum, held, image_grad, done)

    @pl.when(ints[odd] == 0)
    def _():
        text_sum[...] += term("text", GROUP_1, ints, floats, text_unit, [chip], (), partner)
        finish(floats, text, text_sum, held, text_grad, done)


def last_kernel(
    odd, first, final, ints, floats, image, text, partner, image_so_far, text_so_far, link, handed,
    image_done, text_done, image_grad, text_grad, total, held, done,
):
    @pl.when(ints[odd] != 0)
    def _():
        unit = units_of(text[...])[0]
        more = term("text", GROUP_1, ints, floats, unit, [link, handed], (final,), partner)
        total[...] = text_so_far[...] + more
        finish(floats, text, total, held, text_grad, done)

    @pl.when(ints[odd] == 0)
    def _():
        unit = units_of(image[...])[0]
        more = term("image", GROUP_1, ints, floats, unit, [link, handed], (first,), partner)
        total[...] = image_so_far[...] + more
        finish(floats, image, total, held, image_grad, done)


def call(kernel, terms, sums, grads, held, ints, floats, *args, aliased=0):
    rows, width = args[0].shape
    vmem, given = pl.BlockSpec(memory_space=pltpu.VMEM), pl.BlockSpec(memory_space=pl.ANY)
    shape = jax.ShapeDtypeStruct((rows, width), jnp.float32)
    plain = len(args) - aliased
    return pl.pallas_call(
        kernel,
        out_shape=[shape] * (sums + grads),
        in_specs=[pl.BlockSpec(memory_space=pltpu.SMEM)] * 2 + [vmem] * plain + [given] * aliased,
        out_specs=[vmem] * sums + [given] * grads,
        input_output_aliases={2 + plain + n: n for n in range(aliased)},
        scratch_shapes=[pltpu.VMEM((rows, width), jnp.float32)] * held
        + ([pltpu.SemaphoreType.DMA((rows // LAST_ROWS,))] if held else []),
        compiler_params=pltpu.CompilerParams(vmem_limit_bytes=VMEM_LIMIT),
        cost_estimate=pl.CostEstimate(
            flops=4 * terms * rows * rows * width,
            bytes_accessed=12 * terms * rows * width,
            transcendentals=terms * rows * rows,
        ),
    )(ints, floats, *args)


def per_device(image_embed, text_embed, partner, exponent_of_multiplier, logit_bias):
    floats = jnp.concatenate([jnp.exp(exponent_of_multiplier), logit_bias])
    cycle = lax.axis_size("blk")
    groups = lax.axis_size("group")
    rows = image_embed.shape[0]
    g = lax.axis_index("group")
    b = lax.axis_index("blk")

    def send(array, target):
        pairs = []
        for i in range(groups):
            for j in range(cycle):
                to = target(i, j)
                if to is not None:
                    pairs.append((i * cycle + j, (to[0] % groups) * cycle + to[1] % cycle))
        return lax.ppermute(array, ("group", "blk"), pairs)

    def first_of(group_at, cycle_at):
        return (group_at * cycle + cycle_at) * rows

    text_first = [
        first_of(g, (b + cycle - 1) % cycle),
        first_of((g + groups - 1) % groups, b),
        first_of(g, (b + cycle - 2) % cycle),
        first_of(g, b),
    ]
    is_first_group = g == 0
    flags = [is_first_group, g != 0, g % 2 == 1, g % 2 == 0, g == groups - 1]
    ints = jnp.stack(text_first + [flag.astype(jnp.int32) for flag in flags])
    is_first, not_first, is_odd, is_even, is_last = range(4, 9)

    early_text = send(text_embed, lambda i, j: None if i == 0 else (i, j + 1))
    late, link, chip, packed = pack(
        (not_first, is_even, is_odd, None), ints, image_embed, text_embed, partner
    )
    early_image = send(packed, lambda i, j: (i, j - 1) if i == 0 else None)
    packed_again, text_again = lax.optimization_barrier((packed, text_embed))
    x_text = send(text_again, lambda i, j: (i, j + 2))
    x_image = send(packed_again, lambda i, j: (i, j - 2))
    late_in = send(late, lambda i, j: (i, j + 1) if i == 0 else (i, j - 1))
    link, chip, early_text, ints_later = lax.optimization_barrier((link, chip, early_text, ints))
    chip_in = send(chip, lambda i, j: (i ^ 1, j))
    link_in = send(
        link, lambda i, j: None if i in (0, groups - 1) else (i + 1, j) if i % 2 else (i - 1, j)
    )
    own = (image_embed, text_embed, partner[:, None])
    so_far = call(own_kernel, 2, 2, 0, 0, ints_later, floats, *own, packed)
    early_image, *so_far = lax.optimization_barrier((early_image, *so_far))
    so_far = call(x_kernel, 2, 2, 0, 0, ints, floats, *own, *so_far, x_text, x_image)
    handed = send(
        jnp.where(is_first_group, early_image, jnp.pad(early_text, ((0, CODE_ROWS), (0, 0)))),
        lambda i, j: (groups - 1, j + 1) if i == 0 else (0, j - 1) if i == groups - 1 else None,
    )
    kernel = functools.partial(middle_kernel, is_odd, is_first)
    *so_far, image_grad, text_grad = call(
        kernel, 3, 2, 2, 1, ints, floats, *own, *so_far, early_text, early_image, late_in, chip_in
    )
    kernel = functools.partial(last_kernel, is_odd, is_first, is_last)
    return call(
        kernel, 1, 0, 2, 2, ints, floats, *own, *so_far, link_in, handed, image_grad, text_grad, aliased=2
    )


def solution(mesh):
    return jax.shard_map(
        per_device,
        mesh=mesh,
        in_specs=(
            P(("group", "blk"), None),
            P(("group", "blk"), None),
            P(("group", "blk")),
            P(),
            P(),
        ),
        out_specs=(P(("group", "blk"), None), P(("group", "blk"), None)),
        check_vma=False,
    )
```

```python
import functools

import jax
import jax.numpy as jnp
from jax import lax
from jax.experimental import pallas as pl
from jax.experimental.pallas import tpu as pltpu
from jax.sharding import PartitionSpec as P

CODE_ROWS = 16
NO_MATCH = -256.0
VMEM_LIMIT = 32 * 1024 * 1024
LAST_ROWS = 64
BLK_1, GROUP_1, BLK_2, OWN = range(4)


def units_of(values):
    wide = values.astype(jnp.float32)
    scale = lax.rsqrt(jnp.sum(wide * wide, axis=-1, keepdims=True) + 1e-06)
    return wide * scale, scale


def codes_of(ints, partner):
    rows = partner.shape[1]
    row = lax.broadcasted_iota(jnp.int32, (CODE_ROWS, rows), 0)
    codes = jnp.full((CODE_ROWS, rows), NO_MATCH, jnp.float32)
    for kind in range(4):
        place = partner - ints[kind]
        inside = (place >= 0) & (place < rows)
        code = jnp.where(inside, (place - rows // 2).astype(jnp.float32), NO_MATCH)
        codes = jnp.where(row == kind, code, codes)
    return codes


def pack_kernel(flags, ints, image_ref, text_ref, partner_ref, *refs):
    out_refs, done = refs[:-1], refs[-1]
    rows, width = image_ref.shape
    for n, (flag, out_ref) in enumerate(zip(flags, out_refs)):

        def begin(ref, n=n, out_ref=out_ref):
            pltpu.make_async_copy(ref, out_ref.at[:rows, :], done.at[n]).start()

        if flag is None:
            begin(image_ref)
        else:
            pl.when(ints[flag] != 0)(lambda begin=begin: begin(image_ref))
            pl.when(ints[flag] == 0)(lambda begin=begin: begin(text_ref))
    codes = codes_of(ints, partner_ref[...].reshape(1, rows))
    for out_ref in out_refs:
        out_ref[rows:, :rows] = codes.astype(out_ref.dtype)
        out_ref[rows:, rows:] = jnp.zeros((CODE_ROWS, width - rows), out_ref.dtype)
    for n, out_ref in enumerate(out_refs):
        pltpu.make_async_copy(image_ref, out_ref.at[:rows, :], done.at[n]).wait()


def pack(flags, ints, image, text, partner):
    rows, width = image.shape
    vmem, given = pl.BlockSpec(memory_space=pltpu.VMEM), pl.BlockSpec(memory_space=pl.ANY)
    return pl.pallas_call(
        functools.partial(pack_kernel, flags),
        out_shape=[jax.ShapeDtypeStruct((rows + CODE_ROWS, width), jnp.bfloat16)] * len(flags),
        in_specs=[pl.BlockSpec(memory_space=pltpu.SMEM), given, given, vmem],
        out_specs=[vmem] * len(flags),
        scratch_shapes=[pltpu.SemaphoreType.DMA((len(flags),))],
        compiler_params=pltpu.CompilerParams(vmem_limit_bytes=VMEM_LIMIT),
        cost_estimate=pl.CostEstimate(
            flops=rows * width, bytes_accessed=4 * len(flags) * rows * width, transcendentals=0
        ),
    )(ints, image, text, partner)


def term(side, kind, ints, floats, unit, foreign_refs, picks, partner_ref):
    rows = unit.shape[0]
    height = rows if side == "image" else rows + CODE_ROWS
    block = foreign_refs[0][:height, :]
    for other_ref, flag in zip(foreign_refs[1:], picks):
        block = jnp.where(ints[flag] != 0, other_ref[:height, :], block)
    foreign = units_of(block[:rows, :])[0].astype(jnp.bfloat16)
    scores = (
        floats[0]
        * lax.dot_general(
            unit.astype(jnp.bfloat16),
            foreign,
            (((1,), (1,)), ((), ())),
            preferred_element_type=jnp.float32,
        )
        + floats[1]
    )
    if side == "image":
        columns = ints[kind] + lax.broadcasted_iota(jnp.int32, scores.shape, 1)
        matches = partner_ref[...] == columns
    else:
        code = block[rows:, :rows].astype(jnp.float32)[kind : kind + 1, :]
        place = lax.broadcasted_iota(jnp.int32, scores.shape, 0) - rows // 2
        matches = place.astype(jnp.float32) == code
    slope = jax.nn.sigmoid(jnp.where(matches, -scores, scores))
    signal = jnp.where(matches, -slope, slope).astype(jnp.bfloat16)
    return jnp.dot(signal, foreign, preferred_element_type=jnp.float32)


def finish(floats, own_ref, sum_ref, held, out_ref, done):
    copies = []
    for n, start in enumerate(range(0, own_ref.shape[0], LAST_ROWS)):
        here = slice(start, start + LAST_ROWS)
        unit, scale = units_of(own_ref[here, :])
        part = floats[0] * sum_ref[here, :]
        along = jnp.sum(unit * part, axis=-1, keepdims=True)
        held[here, :] = (part - unit * along) * scale
        copies.append(pltpu.make_async_copy(held.at[here, :], out_ref.at[here, :], done.at[n]))
        copies[-1].start()
    for copy in copies:
        copy.wait()


def own_kernel(ints, floats, image, text, partner, packed, image_sum, text_sum):
    image_unit, text_unit = units_of(image[...])[0], units_of(text[...])[0]
    image_sum[...] = term("image", OWN, ints, floats, image_unit, [text], (), partner)
    text_sum[...] = term("text", OWN, ints, floats, text_unit, [packed], (), partner)


def x_kernel(
    ints, floats, image, text, partner, image_so_far, text_so_far, x_text, x_image, image_sum, text_sum
):
    image_unit, text_unit = units_of(image[...])[0], units_of(text[...])[0]
    more = term("image", BLK_2, ints, floats, image_unit, [x_text], (), partner)
    image_sum[...] = image_so_far[...] + more
    more = term("text", BLK_2, ints, floats, text_unit, [x_image], (), partner)
    text_sum[...] = text_so_far[...] + more


def middle_kernel(
    odd, first, ints, floats, image, text, partner, image_so_far, text_so_far, early_text, early_image, late, chip,
    image_sum, text_sum, image_grad, text_grad, held, done,
):
    image_unit, text_unit = units_of(image[...])[0], units_of(text[...])[0]
    more = term("image", BLK_1, ints, floats, image_unit, [early_text, late], (first,), partner)
    image_sum[...] = image_so_far[...] + more
    more = term("text", BLK_1, ints, floats, text_unit, [late, early_image], (first,), partner)
    text_sum[...] = text_so_far[...] + more

    @pl.when(ints[odd] != 0)
    def _():
        image_sum[...] += term("image", GROUP_1, ints, floats, image_unit, [chip], (), partner)
        finish(floats, image, image_sum, held, image_grad, done)

    @pl.when(ints[odd] == 0)
    def _():
        text_sum[...] += term("text", GROUP_1, ints, floats, text_unit, [chip], (), partner)
        finish(floats, text, text_sum, held, text_grad, done)


def last_kernel(
    odd, first, final, ints, floats, image, text, partner, image_so_far, text_so_far, link, handed,
    image_done, text_done, image_grad, text_grad, total, held, done,
):
    @pl.when(ints[odd] != 0)
    def _():
        unit = units_of(text[...])[0]
        more = term("text", GROUP_1, ints, floats, unit, [link, handed], (final,), partner)
        total[...] = text_so_far[...] + more
        finish(floats, text, total, held, text_grad, done)

    @pl.when(ints[odd] == 0)
    def _():
        unit = units_of(image[...])[0]
        more = term("image", GROUP_1, ints, floats, unit, [link, handed], (first,), partner)
        total[...] = image_so_far[...] + more
        finish(floats, image, total, held, image_grad, done)


def call(kernel, terms, sums, grads, held, ints, floats, *args, aliased=0):
    rows, width = args[0].shape
    vmem, given = pl.BlockSpec(memory_space=pltpu.VMEM), pl.BlockSpec(memory_space=pl.ANY)
    shape = jax.ShapeDtypeStruct((rows, width), jnp.float32)
    plain = len(args) - aliased
    return pl.pallas_call(
        kernel,
        out_shape=[shape] * (sums + grads),
        in_specs=[pl.BlockSpec(memory_space=pltpu.SMEM)] * 2 + [vmem] * plain + [given] * aliased,
        out_specs=[vmem] * sums + [given] * grads,
        input_output_aliases={2 + plain + n: n for n in range(aliased)},
        scratch_shapes=[pltpu.VMEM((rows, width), jnp.float32)] * held
        + ([pltpu.SemaphoreType.DMA((rows // LAST_ROWS,))] if held else []),
        compiler_params=pltpu.CompilerParams(vmem_limit_bytes=VMEM_LIMIT),
        cost_estimate=pl.CostEstimate(
            flops=4 * terms * rows * rows * width,
            bytes_accessed=12 * terms * rows * width,
            transcendentals=terms * rows * rows,
        ),
    )(ints, floats, *args)


def per_device(image_embed, text_embed, partner, exponent_of_multiplier, logit_bias):
    floats = jnp.concatenate([jnp.exp(exponent_of_multiplier), logit_bias])
    cycle = lax.axis_size("blk")
    groups = lax.axis_size("group")
    rows = image_embed.shape[0]
    g = lax.axis_index("group")
    b = lax.axis_index("blk")

    def send(array, target):
        pairs = []
        for i in range(groups):
            for j in range(cycle):
                to = target(i, j)
                if to is not None:
                    pairs.append((i * cycle + j, (to[0] % groups) * cycle + to[1] % cycle))
        return lax.ppermute(array, ("group", "blk"), pairs)

    def first_of(group_at, cycle_at):
        return (group_at * cycle + cycle_at) * rows

    text_first = [
        first_of(g, (b + cycle - 1) % cycle),
        first_of((g + groups - 1) % groups, b),
        first_of(g, (b + cycle - 2) % cycle),
        first_of(g, b),
    ]
    is_first_group = g == 0
    flags = [is_first_group, g != 0, g % 2 == 1, g % 2 == 0, g == groups - 1]
    ints = jnp.stack(text_first + [flag.astype(jnp.int32) for flag in flags])
    is_first, not_first, is_odd, is_even, is_last = range(4, 9)

    early_text = send(text_embed, lambda i, j: None if i == 0 else (i, j + 1))
    late, link, chip, packed = pack(
        (not_first, is_even, is_odd, None), ints, image_embed, text_embed, partner
    )
    early_image = send(packed, lambda i, j: (i, j - 1) if i == 0 else None)
    packed_again, text_again = lax.optimization_barrier((packed, text_embed))
    x_text = send(text_again, lambda i, j: (i, j + 2))
    x_image = send(packed_again, lambda i, j: (i, j - 2))
    late_in = send(late, lambda i, j: (i, j + 1) if i == 0 else (i, j - 1))
    link, chip, early_text, ints_later = lax.optimization_barrier((link, chip, early_text, ints))
    chip_in = send(chip, lambda i, j: (i ^ 1, j))
    link_in = send(
        link, lambda i, j: None if i in (0, groups - 1) else (i + 1, j) if i % 2 else (i - 1, j)
    )
    own = (image_embed, text_embed, partner[:, None])
    so_far = call(own_kernel, 2, 2, 0, 0, ints_later, floats, *own, packed)
    early_image, *so_far = lax.optimization_barrier((early_image, *so_far))
    so_far = call(x_kernel, 2, 2, 0, 0, ints, floats, *own, *so_far, x_text, x_image)
    handed = send(
        jnp.where(is_first_group, early_image, jnp.pad(early_text, ((0, CODE_ROWS), (0, 0)))),
        lambda i, j: (groups - 1, j + 1) if i == 0 else (0, j - 1) if i == groups - 1 else None,
    )
    kernel = functools.partial(middle_kernel, is_odd, is_first)
    *so_far, image_grad, text_grad = call(
        kernel, 3, 2, 2, 1, ints, floats, *own, *so_far, early_text, early_image, late_in, chip_in
    )
    kernel = functools.partial(last_kernel, is_odd, is_first, is_last)
    return call(
        kernel, 1, 0, 2, 2, ints, floats, *own, *so_far, link_in, handed, image_grad, text_grad, aliased=2
    )


def solution(mesh):
    return jax.shard_map(
        per_device,
        mesh=mesh,
        in_specs=(
            P(("group", "blk"), None),
            P(("group", "blk"), None),
            P(("group", "blk")),
            P(),
            P(),
        ),
        out_specs=(P(("group", "blk"), None), P(("group", "blk"), None)),
        check_vma=False,
    )
```
